512 devices in a mesh: dp: 16 (over z_lo, x), seq: 32 (over z_hi, y, core).
Axes of the slice: x: 4, y: 4, z: 16 (z_hi: 4, z_lo: 4; z = z_hi * 4 + z_lo), core: 2. Of those that a mesh axis runs over, the one named last changes fastest.
Arguments:
- sequence: bfloat16 [262144, 2048], P(('dp', 'seq')), parts along dimension 0, may hold values from -1.5 to 1.5
- norm_gain: float32 [2048], replicated, may hold values from 0.1 to 1.9
- block_factor: bfloat16 [32, 512, 512], P('seq'), may hold values from -0.25 to 0.25
- twiddle: bfloat16 [5, 2, 16384], P(None, None, 'seq'), may hold values from -0.91 to 0.91
- mlp_gain: float32 [2048], replicated, may hold values from 0.1 to 1.9
- gate_weight: bfloat16 [4, 512, 512], P(None, 'seq'), may hold values from -0.25 to 0.25
- up_weight: bfloat16 [4, 512, 512], P(None, 'seq'), may hold values from -0.25 to 0.25
- down_weight: bfloat16 [4, 512, 512], P(None, 'seq'), may hold values from -0.25 to 0.25
Outputs:
- mixed: bfloat16 [262144, 2048], P(('dp', 'seq')), parts along dimension 0
The draws below stay inside these ranges and needn't reach their ends.
There are 16 independent parts, one for each index of `dp`. The reference program is written for one: setup_inputs(seed, part) draws one part's arguments, and reference() takes and returns one part's arrays. A program takes and returns all parts, laid end to end along the dimension named above; an argument that names none is the same for every part. Nothing has to cross between parts.
All inputs are finite; a program needn't handle non-finite values.
Results may differ from the reference program's by a relative error of at most 0.019.
Values may be sent and summed in bfloat16 or wider, within the bound.
A program may use at most 128 MiB of HBM per device.

```python
import jax
import jax.numpy as jnp
from jax import lax

D = 2048
FF = 2048
NCB = 4
BLK = 512
TOK_DEV = 512
TOKENS = 16384
NBLK = 32
LEVELS = 5


def draw_twiddle(key, part):
    key = jax.random.fold_in(key, 11)
    angle_key, own_key, cross_key = jax.random.split(key, 3)
    spread = jax.random.uniform(angle_key, (LEVELS, TOKENS), jnp.float32)
    angles = 0.45 + 0.67 * spread
    own_sign = 2.0 * jax.random.randint(own_key, (LEVELS, TOKENS), 0, 2).astype(jnp.float32) - 1.0
    cross_sign = 2.0 * jax.random.randint(cross_key, (LEVELS, TOKENS), 0, 2).astype(jnp.float32) - 1.0
    stacked = jnp.stack([own_sign * jnp.cos(angles), cross_sign * jnp.sin(angles)], axis=1)
    return stacked.astype(jnp.bfloat16)


def steps_of(stream_key, shape, shards, least, high):
    level, own = 1.0, jax.random.fold_in(stream_key, 6)
    for position, blocks in shards:
        heights = jnp.exp(jax.random.uniform(jax.random.fold_in(own, position), (blocks,), jnp.float32, least / len(shards), high / len(shards)))
        level = level * jnp.repeat(heights, shape[position] // blocks).reshape([-1 if axis == position else 1 for axis in range(len(shape))])
    return level


def noise(rng, extent, scale, most, cuts=(), dtype=jnp.bfloat16):
    array = jax.random.normal(rng, extent, jnp.float32) * scale
    if len(cuts) > 0:
        array = steps_of(rng, extent, cuts, -0.22, 0.18) * array
    return jnp.clip(array, min=-most, max=most).astype(dtype)


def setup_inputs(seed: int = 0, part: int = 0) -> dict:
    key_of = jax.random.split(jax.random.key(seed), 9)
    part_splits = jax.random.split(jax.random.fold_in(key_of[8], part), 9)
    return {
        "sequence": noise(part_splits[0], (TOKENS, D), 0.25, 1.5, ((0, 32),)),
        "norm_gain": jnp.clip(1.0 + 0.18 * jax.random.normal(key_of[1], (D,), jnp.float32), 0.1, 1.9),
        "block_factor": noise(key_of[2], (NBLK, BLK, BLK), BLK ** -0.5, 0.25, ((0, 32),)),
        "twiddle": draw_twiddle(jax.random.fold_in(key_of[8], 71), part),
        "mlp_gain": jnp.clip(1.0 + 0.18 * jax.random.normal(key_of[4], (D,), jnp.float32), 0.1, 1.9),
        "gate_weight": noise(key_of[5], (NCB, D // NCB, FF // NCB), (D // NCB) ** -0.5, 0.25, ((1, 32),)),
        "up_weight": noise(key_of[6], (NCB, D // NCB, FF // NCB), (D // NCB) ** -0.5, 0.25, ((1, 32),)),
        "down_weight": noise(key_of[7], (NCB, FF // NCB, D // NCB), (FF // NCB) ** -0.5, 0.25, ((1, 32),)),
    }


def rms_norm(values, scales):
    floats = values.astype(jnp.float32)
    mean_sq = lax.optimization_barrier(jnp.mean(floats * floats, axis=-1, keepdims=True))
    return (floats * lax.rsqrt(mean_sq + 1e-06) * scales.astype(jnp.float32)).astype(jnp.bfloat16)

def reference(sequence, norm_gain, block_factor, twiddle, mlp_gain, gate_weight, up_weight, down_weight):
    normed = rms_norm(sequence, norm_gain)
    blocks = normed.astype(jnp.float32).reshape(NBLK, BLK, D)
    local_mix = jnp.einsum('bij,bjd->bid', block_factor.astype(jnp.float32), blocks)
    current = local_mix.reshape(TOKENS, D).astype(jnp.bfloat16)
    for section_index in range(LEVELS):
        stride_rows = TOK_DEV * 2 ** section_index
        grouped = current.astype(jnp.float32).reshape(TOKENS // (2 * stride_rows), 2, stride_rows, D)
        partner = grouped[:, ::-1].reshape(TOKENS, D)
        own_coef = twiddle[section_index, 0].astype(jnp.float32)[:, None]
        cross_coef = twiddle[section_index, 1].astype(jnp.float32)[:, None]
        current = (own_coef * current.astype(jnp.float32) + cross_coef * partner).astype(jnp.bfloat16)
    residual = (sequence.astype(jnp.float32) + current.astype(jnp.float32)).astype(jnp.bfloat16)
    normed_two = rms_norm(residual, mlp_gain)
    groups = normed_two.astype(jnp.float32).reshape(TOKENS, NCB, D // NCB)
    gate_act = jnp.einsum('tkc,kcf->tkf', groups, gate_weight.astype(jnp.float32))
    up_act = jnp.einsum('tkc,kcf->tkf', groups, up_weight.astype(jnp.float32))
    hidden = (jax.nn.silu(gate_act) * up_act).astype(jnp.bfloat16)
    down_out = jnp.einsum('tkf,kfc->tkc', hidden.astype(jnp.float32), down_weight.astype(jnp.float32))
    return (residual.astype(jnp.float32) + down_out.reshape(TOKENS, D)).astype(jnp.bfloat16)
```

```python
import functools

import jax
import jax.numpy as jnp
from jax import lax
from jax.experimental import pallas as pl
from jax.experimental.pallas import tpu as pltpu
from jax.sharding import PartitionSpec as P

MESH = pl.DeviceIdType.MESH
F32 = jnp.float32
BF16 = jnp.bfloat16

ZH = 4
YN = 4
XN = 4
ROWS = 512
FEAT = 2048
GRP = 512
CH = 8
R = 16
TILE = 512


def flip1(v):
    return v + 1 - 2 * (v % 2)


def flip2(v):
    return v + 2 - 4 * ((v // 2) % 2)


def flips(v):
    return (flip1(v), flip2(v), 3 - v)


def remote(src, dst, send, recv, device):
    return pltpu.make_async_remote_copy(
        src_ref=src,
        dst_ref=dst,
        send_sem=send,
        recv_sem=recv,
        device_id=device,
        device_id_type=MESH,
    )


def kernel(
    seq_hbm,
    ngain_ref,
    bf_hbm,
    tw_ref,
    mgain_ref,
    gw_hbm,
    uw_hbm,
    dw_hbm,
    out_hbm,
    seq,
    bf,
    normed,
    zs,
    z1,
    cr,
    c1,
    y1,
    c2,
    y2,
    ob,
    z2,
    wt,
    tws,
    twr,
    twt,
    xs,
    res,
    outb,
    seq_sem,
    bf_sem,
    w_sem,
    out_sem,
    tw_send,
    tw_recv,
    wz_send,
    wz_recv,
    wy_send,
    wy_recv,
    wx_send,
    wx_recv,
    wc_send,
    wc_recv,
    z1_send,
    z1_recv,
    cr_send,
    cr_recv,
    y1_send,
    y1_recv,
    y2_send,
    y2_recv,
    z2_send,
    z2_recv,
):
    dp = lax.axis_index("dp")
    sq = lax.axis_index("seq")
    zl, xx = dp // XN, dp % XN
    zh, yy, cc = sq // (YN * 2), (sq // 2) % YN, sq % 2

    def place(z=None, y=None, c=None, x=None):
        z = zh if z is None else z
        y = yy if y is None else y
        c = cc if c is None else c
        x = xx if x is None else x
        return (zl * XN + x, z * (YN * 2) + y * 2 + c)

    zp = flips(zh)
    yp = flips(yy)
    xp = flips(xx)
    cp = 1 - cc

    barrier = pltpu.get_barrier_semaphore()
    peers = (
        [place(z=z) for z in zp]
        + [place(y=y) for y in yp]
        + [place(x=x) for x in xp]
        + [place(c=cp)]
    )
    for peer in peers:
        pl.semaphore_signal(barrier, inc=1, device_id=peer, device_id_type=MESH)

    seq_copies = []
    for i in range(4):
        rows = pl.ds(i * 128, 128)
        copy = pltpu.make_async_copy(seq_hbm.at[rows], seq.at[rows], seq_sem.at[i])
        copy.start()
        seq_copies.append(copy)
    bf_copy = pltpu.make_async_copy(bf_hbm.at[0], bf, bf_sem)
    bf_copy.start()
    w_copies = []
    for m, w_hbm in enumerate((gw_hbm, uw_hbm, dw_hbm)):
        copy = pltpu.make_async_copy(
            w_hbm.at[xx], wt.at[xx, zh, yy, cc, pl.ds(m * 16, 16)], w_sem.at[m]
        )
        copy.start()
        w_copies.append(copy)
    for s in range(5):
        tws[pl.ds(2 * s, 2), :] = tw_ref[s].astype(F32)
    tws[pl.ds(10, 6), :] = jnp.zeros((6, ROWS), F32)
    twr[zh] = tws[:, pl.ds(pl.multiple_of(zh * 128, 128), 128)]
    for copy in w_copies:
        copy.wait()

    pl.semaphore_wait(barrier, len(peers))

    wz, tz = [], []
    for i, z in enumerate(zp):
        own = wt.at[xx, zh, yy, cc]
        copy = remote(own, own, wz_send.at[i], wz_recv.at[i], place(z=z))
        copy.start()
        wz.append(copy)
        copy = remote(
            tws.at[:, pl.ds(pl.multiple_of(z * 128, 128), 128)],
            twr.at[zh],
            tw_send.at[i],
            tw_recv.at[i],
            place(z=z),
        )
        copy.start()
        tz.append(copy)

    for i in range(4):
        seq_copies[i].wait()

        @pl.loop(0, 8)
        def _(j):
            rows = pl.ds(pl.multiple_of(i * 128 + j * 16, 16), 16)
            v = seq[rows, :].astype(F32)
            scale = lax.rsqrt(jnp.mean(v * v, axis=-1, keepdims=True) + 1e-6)
            normed[rows, :] = (v * scale * ngain_ref[...]).astype(BF16)

    bf_copy.wait()

    def z1_copy(c, i):
        return remote(
            zs.at[c, zp[i]], z1.at[c, zh], z1_send.at[c, i], z1_recv.at[c, i], place(z=zp[i])
        )

    @pl.loop(0, CH)
    def _(c):
        lhs = jnp.concatenate(
            [bf[pl.ds(pl.multiple_of(q * 128 + c * R, R), R), :] for q in range(ZH)], axis=0
        )
        for n in range(FEAT // TILE):
            cols = pl.ds(n * TILE, TILE)
            mix = jnp.dot(lhs, normed[:, cols], preferred_element_type=F32).astype(BF16)
            zs[c, :, :, cols] = mix.reshape(ZH, R, TILE)
        for i in range(3):
            z1_copy(c, i).start()
        z1[c, zh] = zs[c, zh]

    for copy in wz:
        copy.wait_recv()
    wy = []
    for i, y in enumerate(yp):
        own = wt.at[xx, :, yy, cc]
        copy = remote(own, own, wy_send.at[i], wy_recv.at[i], place(y=y))
        copy.start()
        wy.append(copy)

    for copy in tz:
        copy.wait_recv()
    for z in range(ZH):
        block = jnp.concatenate([twr[z], jnp.zeros((112, 128), F32)], axis=0)
        twt[z] = block.T

    def c_copy(c):
        return remote(z1.at[c], cr.at[c], cr_send.at[c], cr_recv.at[c], place(c=cp))

    def y1_copy(c):
        return remote(c1.at[c], y1.at[c], y1_send.at[c], y1_recv.at[c], place(y=yp[0]))

    def y2_copy(c):
        return remote(c2.at[c], y2.at[c], y2_send.at[c], y2_recv.at[c], place(y=yp[1]))

    def z2_copy(c, i):
        return remote(
            ob.at[c, zp[i]], z2.at[c, zh], z2_send.at[c, i], z2_recv.at[c, i], place(z=zp[i])
        )

    def coefs(c, z, s):
        rows = pl.ds(pl.multiple_of(c * R, R), R)
        block = twt[z, rows, :]
        return block[:, 2 * s : 2 * s + 1], block[:, 2 * s + 1 : 2 * s + 2]

    def section(c, s, cur, other, to):
        for z in range(ZH):
            own, cross = coefs(c, z, s)
            for n in range(FEAT // TILE):
                cols = pl.ds(n * TILE, TILE)
                to[c, z, :, cols] = (
                    own * cur[c, z, :, cols].astype(F32)
                    + cross * other[c, z, :, cols].astype(F32)
                ).astype(BF16)

    def last_sections(c):
        pairs = [[coefs(c, z, s) for z in range(ZH)] for s in (2, 3, 4)]
        for n in range(FEAT // 256):
            cols = pl.ds(n * 256, 256)
            cur = [
                (
                    pairs[0][z][0] * c2[c, z, :, cols].astype(F32)
                    + pairs[0][z][1] * y2[c, z, :, cols].astype(F32)
                )
                .astype(BF16)
                .astype(F32)
                for z in range(ZH)
            ]
            for s, step in ((1, 1), (2, 2)):
                cur = [
                    (pairs[s][z][0] * cur[z] + pairs[s][z][1] * cur[z ^ step])
                    .astype(BF16)
                    .astype(F32)
                    for z in range(ZH)
                ]
            for z in range(ZH):
                ob[c, z, :, cols] = cur[z].astype(BF16)

    @pl.loop(0, CH + 2)
    def _(t):
        @pl.when(t < CH)
        def _():
            for i in range(3):
                z1_copy(t, i).wait_recv()
            c_copy(t).start()

        @pl.when(t >= 2)
        def _():
            c = t - 2
            y2_copy(c).wait_recv()
            last_sections(c)
            for i in range(3):
                z2_copy(c, i).start()
            z2[c, zh] = ob[c, zh]

        @pl.when((t >= 1) & (t < CH + 1))
        def _():
            c = t - 1
            y1_copy(c).wait_recv()
            section(c, 1, c1, y1, c2)
            y2_copy(c).start()

        @pl.when(t < CH)
        def _():
            c_copy(t).wait_recv()
            section(t, 0, z1, cr, c1)
            y1_copy(t).start()

        @pl.when(t == 2)
        def _():
            for i in range(3):
                own = wt.at[xx, :, yy, cc]
                remote(own, own, wy_send.at[i], wy_recv.at[i], place(y=yp[i])).wait_recv()
            for i in range(3):
                own = wt.at[xx, :, :, cc]
                remote(own, own, wx_send.at[i], wx_recv.at[i], place(x=xp[i])).start()

        @pl.when(t == CH + 1)
        def _():
            for i in range(3):
                own = wt.at[xx, :, :, cc]
                remote(own, own, wx_send.at[i], wx_recv.at[i], place(x=xp[i])).wait_recv()
            own = wt.at[:, :, :, cc]
            remote(own, own, wc_send, wc_recv, place(c=cp)).start()

    own = wt.at[:, :, :, cc]
    w_core = remote(own, own, wc_send, wc_recv, place(c=cp))
    w_core.wait_recv()

    def weight(k, m):
        return wt[k, :, :, :, m * 16 : (m + 1) * 16, :].reshape(GRP, GRP)

    def out_copy(c, q):
        rows = pl.ds(pl.multiple_of(q * 128 + c * R, R), R)
        return pltpu.make_async_copy(outb.at[c, q], out_hbm.at[rows], out_sem.at[c, q])

    @pl.loop(0, CH)
    def _(c):
        for i in range(3):
            z2_copy(c, i).wait_recv()
        for q in range(ZH):
            rows = pl.ds(pl.multiple_of(q * 128 + c * R, R), R)
            r = (seq[rows, :].astype(F32) + z2[c, q].astype(F32)).astype(BF16)
            res[pl.ds(q * R, R), :] = r
            v = r.astype(F32)
            scale = lax.rsqrt(jnp.mean(v * v, axis=-1, keepdims=True) + 1e-6)
            xs[pl.ds(q * R, R), :] = (v * scale * mgain_ref[...]).astype(BF16)

        for k in range(FEAT // GRP):
            cols = pl.ds(k * GRP, GRP)
            x = xs[:, cols]
            gate = jnp.dot(x, weight(k, 0), preferred_element_type=F32)
            up = jnp.dot(x, weight(k, 1), preferred_element_type=F32)
            hidden = (gate / (1.0 + jnp.exp(-gate)) * up).astype(BF16)
            down = jnp.dot(hidden, weight(k, 2), preferred_element_type=F32)
            mixed = (res[:, cols].astype(F32) + down).astype(BF16)
            outb[c, :, :, cols] = mixed.reshape(ZH, R, GRP)
        for q in range(ZH):
            out_copy(c, q).start()

    for copy in wz + wy + tz:
        copy.wait_send()
    for i in range(3):
        own = wt.at[xx, :, :, cc]
        remote(own, own, wx_send.at[i], wx_recv.at[i], place(x=xp[i])).wait_send()
    w_core.wait_send()

    @pl.loop(0, CH)
    def _(c):
        for i in range(3):
            z1_copy(c, i).wait_send()
            z2_copy(c, i).wait_send()
        c_copy(c).wait_send()
        y1_copy(c).wait_send()
        y2_copy(c).wait_send()
        for q in range(ZH):
            out_copy(c, q).wait()


def local(
    sequence, norm_gain, block_factor, twiddle, mlp_gain, gate_weight, up_weight, down_weight
):
    any_space = pl.BlockSpec(memory_space=pl.ANY)
    vmem = pl.BlockSpec(memory_space=pltpu.VMEM)
    chunk = pltpu.VMEM((CH, ZH, R, FEAT), BF16)
    dma = pltpu.SemaphoreType.DMA
    return pl.pallas_call(
        kernel,
        name="monarch",
        out_shape=jax.ShapeDtypeStruct((ROWS, FEAT), BF16),
        in_specs=[any_space, vmem, any_space, vmem, vmem, any_space, any_space, any_space],
        out_specs=any_space,
        scratch_shapes=[
            pltpu.VMEM((ROWS, FEAT), BF16),
            pltpu.VMEM((ROWS, ROWS), BF16),
            pltpu.VMEM((ROWS, FEAT), BF16),
            chunk,
            chunk,
            chunk,
            chunk,
            chunk,
            chunk,
            chunk,
            chunk,
            chunk,
            pltpu.VMEM((XN, ZH, YN, 2, 48, GRP), BF16),
            pltpu.VMEM((16, ROWS), F32),
            pltpu.VMEM((ZH, 16, 128), F32),
            pltpu.VMEM((ZH, 128, 128), F32),
            pltpu.VMEM((ZH * R, FEAT), BF16),
            pltpu.VMEM((ZH * R, FEAT), BF16),
            chunk,
            dma((4,)),
            dma,
            dma((3,)),
            dma((CH, ZH)),
            dma((3,)),
            dma((3,)),
            dma((3,)),
            dma((3,)),
            dma((3,)),
            dma((3,)),
            dma((3,)),
            dma((3,)),
            dma,
            dma,
            dma((CH, 3)),
            dma((CH, 3)),
            dma((CH,)),
            dma((CH,)),
            dma((CH,)),
            dma((CH,)),
            dma((CH,)),
            dma((CH,)),
            dma((CH, 3)),
            dma((CH, 3)),
        ],
        compiler_params=pltpu.CompilerParams(
            collective_id=0, has_side_effects=True, vmem_limit_bytes=56 * 1024 * 1024
        ),
        cost_estimate=pl.CostEstimate(
            flops=5 * 2**30, bytes_accessed=8 * 2**20, transcendentals=2**20
        ),
    )(
        sequence,
        norm_gain.reshape(1, FEAT),
        block_factor,
        twiddle,
        mlp_gain.reshape(1, FEAT),
        gate_weight,
        up_weight,
        down_weight,
    )


def solution(mesh):
    return jax.shard_map(
        local,
        mesh=mesh,
        in_specs=(
            P(("dp", "seq"), None),
            P(),
            P("seq", None, None),
            P(None, None, "seq"),
            P(),
            P(None, "seq", None),
            P(None, "seq", None),
            P(None, "seq", None),
        ),
        out_specs=P(("dp", "seq"), None),
        check_vma=False,
    )
```

```python
import functools

import jax
import jax.numpy as jnp
from jax import lax
from jax.experimental import pallas as pl
from jax.experimental.pallas import tpu as pltpu
from jax.sharding import PartitionSpec as P

MESH = pl.DeviceIdType.MESH
F32 = jnp.float32
BF16 = jnp.bfloat16

ZH = 4
YN = 4
XN = 4
ROWS = 512
FEAT = 2048
GRP = 512
CH = 8
R = 16
TILE = 512
YC = 512


def flip1(v):
    return v + 1 - 2 * (v % 2)


def flip2(v):
    return v + 2 - 4 * ((v // 2) % 2)


def flips(v):
    return (flip1(v), flip2(v), 3 - v)


def remote(src, dst, send, recv, device):
    return pltpu.make_async_remote_copy(
        src_ref=src,
        dst_ref=dst,
        send_sem=send,
        recv_sem=recv,
        device_id=device,
        device_id_type=MESH,
    )


def kernel(
    seq_hbm,
    ngain_ref,
    bf_hbm,
    tw_ref,
    mgain_ref,
    gw_hbm,
    uw_hbm,
    dw_hbm,
    out_hbm,
    seq,
    bf,
    normed,
    zs,
    z1,
    cr,
    c1,
    ya,
    yo,
    ob,
    z2,
    wt,
    tws,
    twr,
    twy,
    twt,
    xs,
    res,
    outb,
    seq_sem,
    bf_sem,
    w_sem,
    out_sem,
    tw_send,
    tw_recv,
    ty_send,
    ty_recv,
    wz_send,
    wz_recv,
    wy_send,
    wy_recv,
    wx_send,
    wx_recv,
    wc_send,
    wc_recv,
    z1_send,
    z1_recv,
    cr_send,
    cr_recv,
    ya_send,
    ya_recv,
    yo_send,
    yo_recv,
    z2_send,
    z2_recv,
):
    dp = lax.axis_index("dp")
    sq = lax.axis_index("seq")
    zl, xx = dp // XN, dp % XN
    zh, yy, cc = sq // (YN * 2), (sq // 2) % YN, sq % 2

    def place(z=None, y=None, c=None, x=None):
        z = zh if z is None else z
        y = yy if y is None else y
        c = cc if c is None else c
        x = xx if x is None else x
        return (zl * XN + x, z * (YN * 2) + y * 2 + c)

    zp = flips(zh)
    yp = flips(yy)
    xp = flips(xx)
    cp = 1 - cc

    barrier = pltpu.get_barrier_semaphore()
    peers = (
        [place(z=z) for z in zp]
        + [place(y=y) for y in yp]
        + [place(x=x) for x in xp]
        + [place(c=cp)]
    )
    for peer in peers:
        pl.semaphore_signal(barrier, inc=1, device_id=peer, device_id_type=MESH)

    seq_copies = []
    for i in range(4):
        rows = pl.ds(i * 128, 128)
        copy = pltpu.make_async_copy(seq_hbm.at[rows], seq.at[rows], seq_sem.at[i])
        copy.start()
        seq_copies.append(copy)
    bf_copy = pltpu.make_async_copy(bf_hbm.at[0], bf, bf_sem)
    bf_copy.start()
    w_copies = []
    for m, w_hbm in enumerate((gw_hbm, uw_hbm, dw_hbm)):
        copy = pltpu.make_async_copy(
            w_hbm.at[xx], wt.at[xx, zh, yy, cc, pl.ds(m * 16, 16)], w_sem.at[m]
        )
        copy.start()
        w_copies.append(copy)
    for s in range(5):
        tws[pl.ds(2 * s, 2), :] = tw_ref[s].astype(F32)
    tws[pl.ds(10, 6), :] = jnp.zeros((6, ROWS), F32)
    twr[zh] = tws[:, pl.ds(pl.multiple_of(zh * 128, 128), 128)]
    for copy in w_copies:
        copy.wait()

    pl.semaphore_wait(barrier, len(peers))

    wz, tz = [], []
    for i, z in enumerate(zp):
        own = wt.at[xx, zh, yy, cc]
        copy = remote(own, own, wz_send.at[i], wz_recv.at[i], place(z=z))
        copy.start()
        wz.append(copy)
        copy = remote(
            tws.at[:, pl.ds(pl.multiple_of(z * 128, 128), 128)],
            twr.at[zh],
            tw_send.at[i],
            tw_recv.at[i],
            place(z=z),
        )
        copy.start()
        tz.append(copy)

    for i in range(4):
        seq_copies[i].wait()

        @pl.loop(0, 8, unroll=4)
        def _(j):
            rows = pl.ds(pl.multiple_of(i * 128 + j * 16, 16), 16)
            v = seq[rows, :].astype(F32)
            scale = lax.rsqrt(jnp.mean(v * v, axis=-1, keepdims=True) + 1e-6)
            normed[rows, :] = (v * scale * ngain_ref[...]).astype(BF16)

    bf_copy.wait()

    def z1_copy(c, i):
        return remote(
            zs.at[c, zp[i]], z1.at[c, zh], z1_send.at[c, i], z1_recv.at[c, i], place(z=zp[i])
        )

    @pl.loop(0, CH)
    def _(c):
        lhs = jnp.concatenate(
            [bf[pl.ds(pl.multiple_of(q * 128 + c * R, R), R), :] for q in range(ZH)], axis=0
        )
        for n in range(FEAT // TILE):
            cols = pl.ds(n * TILE, TILE)
            mix = jnp.dot(lhs, normed[:, cols], preferred_element_type=F32).astype(BF16)
            zs[c, :, :, cols] = mix.reshape(ZH, R, TILE)
        for i in range(3):
            z1_copy(c, i).start()
        z1[c, zh] = zs[c, zh]

    for copy in wz:
        copy.wait_recv()
    wy = []
    for i, y in enumerate(yp):
        own = wt.at[xx, :, yy, cc]
        copy = remote(own, own, wy_send.at[i], wy_recv.at[i], place(y=y))
        copy.start()
        wy.append(copy)
    for copy in tz:
        copy.wait_recv()
    ty = []
    for i, y in enumerate(yp):
        copy = remote(twr, twy.at[yy], ty_send.at[i], ty_recv.at[i], place(y=y))
        copy.start()
        ty.append(copy)
    twy[yy] = twr[...]
    for copy in ty:
        copy.wait_recv()
    for h in range(2):
        twt[h] = twy[2 * h : 2 * h + 2].reshape(128, 128).T
    twt[2] = jnp.concatenate([twr[...].reshape(64, 128), jnp.zeros((64, 128), F32)], axis=0).T

    def c_copy(c):
        return remote(z1.at[c], cr.at[c], cr_send.at[c], cr_recv.at[c], place(c=cp))

    def ya_copy(c, i):
        cols = pl.ds(pl.multiple_of(yp[i] * YC, YC), YC)
        return remote(
            c1.at[c, :, :, cols],
            ya.at[c, yy],
            ya_send.at[c, i],
            ya_recv.at[c, i],
            place(y=yp[i]),
        )

    def yo_copy(c, i):
        cols = pl.ds(pl.multiple_of(yy * YC, YC), YC)
        return remote(
            yo.at[c, yp[i]],
            ob.at[c, :, :, cols],
            yo_send.at[c, i],
            yo_recv.at[c, i],
            place(y=yp[i]),
        )

    def z2_copy(c, i):
        return remote(
            ob.at[c, zp[i]], z2.at[c, zh], z2_send.at[c, i], z2_recv.at[c, i], place(z=zp[i])
        )

    mine = pl.ds(pl.multiple_of(yy * YC, YC), YC)

    def first_section(c):
        block = twt[2, pl.ds(pl.multiple_of(c * R, R), R), :]
        for z in range(ZH):
            own, cross = block[:, 16 * z : 16 * z + 1], block[:, 16 * z + 1 : 16 * z + 2]
            for n in range(FEAT // TILE):
                cols = pl.ds(n * TILE, TILE)
                c1[c, z, :, cols] = (
                    own * z1[c, z, :, cols].astype(F32) + cross * cr[c, z, :, cols].astype(F32)
                ).astype(BF16)

    def other_sections(c):
        rows = pl.ds(pl.multiple_of(c * R, R), R)
        blocks = (twt[0, rows, :], twt[1, rows, :])

        def coefs(b, s):
            lane = (b % 8) * 16 + 2 * s
            return blocks[b // 8][:, lane : lane + 1], blocks[b // 8][:, lane + 1 : lane + 2]

        for n in range(YC // 128):
            cols = pl.ds(n * 128, 128)
            cur = [ya[c, b // ZH, b % ZH, :, cols].astype(F32) for b in range(YN * ZH)]
            for s, step in ((1, 4), (2, 8), (3, 1), (4, 2)):
                to = []
                for b in range(YN * ZH):
                    own, cross = coefs(b, s)
                    to.append((own * cur[b] + cross * cur[b ^ step]).astype(BF16))
                cur = to if s == 4 else [v.astype(F32) for v in to]
            for b in range(YN * ZH):
                yo[c, b // ZH, b % ZH, :, cols] = cur[b]

    @pl.loop(0, CH + 2)
    def _(t):
        @pl.when(t < CH)
        def _():
            for i in range(3):
                z1_copy(t, i).wait_recv()
            c_copy(t).start()

        @pl.when(t >= 2)
        def _():
            c = t - 2
            for i in range(3):
                yo_copy(c, i).wait_recv()
            for i in range(3):
                z2_copy(c, i).start()
            z2[c, zh] = ob[c, zh]

        @pl.when((t >= 1) & (t < CH + 1))
        def _():
            c = t - 1
            for i in range(3):
                ya_copy(c, i).wait_recv()
            other_sections(c)
            for i in range(3):
                yo_copy(c, i).start()
            ob[c, :, :, mine] = yo[c, yy]

        @pl.when(t < CH)
        def _():
            c_copy(t).wait_recv()
            first_section(t)
            for i in range(3):
                ya_copy(t, i).start()
            ya[t, yy] = c1[t, :, :, mine]

        @pl.when(t == 1)
        def _():
            for i in range(3):
                own = wt.at[xx, :, yy, cc]
                remote(own, own, wy_send.at[i], wy_recv.at[i], place(y=yp[i])).wait_recv()
            for i in range(3):
                own = wt.at[xx, :, :, cc]
                remote(own, own, wx_send.at[i], wx_recv.at[i], place(x=xp[i])).start()

        @pl.when(t == 6)
        def _():
            for i in range(3):
                own = wt.at[xx, :, :, cc]
                remote(own, own, wx_send.at[i], wx_recv.at[i], place(x=xp[i])).wait_recv()
            own = wt.at[:, :, :, cc]
            remote(own, own, wc_send, wc_recv, place(c=cp)).start()

    own = wt.at[:, :, :, cc]
    w_core = remote(own, own, wc_send, wc_recv, place(c=cp))
    w_core.wait_recv()

    def weight(k, m):
        return wt[k, :, :, :, m * 16 : (m + 1) * 16, :].reshape(GRP, GRP)

    def out_copy(c, q):
        rows = pl.ds(pl.multiple_of(q * 128 + c * R, R), R)
        return pltpu.make_async_copy(outb.at[c, q], out_hbm.at[rows], out_sem.at[c, q])

    @pl.loop(0, CH)
    def _(c):
        for i in range(3):
            z2_copy(c, i).wait_recv()
        for q in range(ZH):
            rows = pl.ds(pl.multiple_of(q * 128 + c * R, R), R)
            r = (seq[rows, :].astype(F32) + z2[c, q].astype(F32)).astype(BF16)
            res[pl.ds(q * R, R), :] = r
            v = r.astype(F32)
            scale = lax.rsqrt(jnp.mean(v * v, axis=-1, keepdims=True) + 1e-6)
            xs[pl.ds(q * R, R), :] = (v * scale * mgain_ref[...]).astype(BF16)

        for k in range(FEAT // GRP):
            cols = pl.ds(k * GRP, GRP)
            x = xs[:, cols]
            gate = jnp.dot(x, weight(k, 0), preferred_element_type=F32)
            up = jnp.dot(x, weight(k, 1), preferred_element_type=F32)
            hidden = (gate / (1.0 + jnp.exp(-gate)) * up).astype(BF16)
            down = jnp.dot(hidden, weight(k, 2), preferred_element_type=F32)
            mixed = (res[:, cols].astype(F32) + down).astype(BF16)
            outb[c, :, :, cols] = mixed.reshape(ZH, R, GRP)
        for q in range(ZH):
            out_copy(c, q).start()

    for copy in wz + wy + tz + ty:
        copy.wait_send()
    for i in range(3):
        own = wt.at[xx, :, :, cc]
        remote(own, own, wx_send.at[i], wx_recv.at[i], place(x=xp[i])).wait_send()
    w_core.wait_send()

    @pl.loop(0, CH)
    def _(c):
        for i in range(3):
            z1_copy(c, i).wait_send()
            z2_copy(c, i).wait_send()
        c_copy(c).wait_send()
        for i in range(3):
            ya_copy(c, i).wait_send()
            yo_copy(c, i).wait_send()
        for q in range(ZH):
            out_copy(c, q).wait()


def local(
    sequence, norm_gain, block_factor, twiddle, mlp_gain, gate_weight, up_weight, down_weight
):
    any_space = pl.BlockSpec(memory_space=pl.ANY)
    vmem = pl.BlockSpec(memory_space=pltpu.VMEM)
    chunk = pltpu.VMEM((CH, ZH, R, FEAT), BF16)
    dma = pltpu.SemaphoreType.DMA
    return pl.pallas_call(
        kernel,
        name="monarch",
        out_shape=jax.ShapeDtypeStruct((ROWS, FEAT), BF16),
        in_specs=[any_space, vmem, any_space, vmem, vmem, any_space, any_space, any_space],
        out_specs=any_space,
        scratch_shapes=[
            pltpu.VMEM((ROWS, FEAT), BF16),
            pltpu.VMEM((ROWS, ROWS), BF16),
            pltpu.VMEM((ROWS, FEAT), BF16),
            chunk,
            chunk,
            chunk,
            chunk,
            pltpu.VMEM((CH, YN, ZH, R, YC), BF16),
            pltpu.VMEM((CH, YN, ZH, R, YC), BF16),
            chunk,
            chunk,
            pltpu.VMEM((XN, ZH, YN, 2, 48, GRP), BF16),
            pltpu.VMEM((16, ROWS), F32),
            pltpu.VMEM((ZH, 16, 128), F32),
            pltpu.VMEM((YN, ZH, 16, 128), F32),
            pltpu.VMEM((3, 128, 128), F32),
            pltpu.VMEM((ZH * R, FEAT), BF16),
            pltpu.VMEM((ZH * R, FEAT), BF16),
            chunk,
            dma((4,)),
            dma,
            dma((3,)),
            dma((CH, ZH)),
            dma((3,)),
            dma((3,)),
            dma((3,)),
            dma((3,)),
            dma((3,)),
            dma((3,)),
            dma((3,)),
            dma((3,)),
            dma((3,)),
            dma((3,)),
            dma,
            dma,
            dma((CH, 3)),
            dma((CH, 3)),
            dma((CH,)),
            dma((CH,)),
            dma((CH, 3)),
            dma((CH, 3)),
            dma((CH, 3)),
            dma((CH, 3)),
            dma((CH, 3)),
            dma((CH, 3)),
        ],
        compiler_params=pltpu.CompilerParams(
            collective_id=0, has_side_effects=True, vmem_limit_bytes=56 * 1024 * 1024
        ),
        cost_estimate=pl.CostEstimate(
            flops=5 * 2**30, bytes_accessed=8 * 2**20, transcendentals=2**20
        ),
    )(
        sequence,
        norm_gain.reshape(1, FEAT),
        block_factor,
        twiddle,
        mlp_gain.reshape(1, FEAT),
        gate_weight,
        up_weight,
        down_weight,
    )


def solution(mesh):
    return jax.shard_map(
        local,
        mesh=mesh,
        in_specs=(
            P(("dp", "seq"), None),
            P(),
            P("seq", None, None),
            P(None, None, "seq"),
            P(),
            P(None, "seq", None),
            P(None, "seq", None),
            P(None, "seq", None),
        ),
        out_specs=P(("dp", "seq"), None),
        check_vma=False,
    )
```

```python
import functools

import jax
import jax.numpy as jnp
from jax import lax
from jax.experimental import pallas as pl
from jax.experimental.pallas import tpu as pltpu
from jax.sharding import PartitionSpec as P

MESH = pl.DeviceIdType.MESH
F32 = jnp.float32
BF16 = jnp.bfloat16

ZH = 4
ZL = 4
YN = 4
XN = 4
ROWS = 512
FEAT = 2048
GRP = 512
CH = 8
R = 16
TILE = 512
YC = 512


def flip1(v):
    return v + 1 - 2 * (v % 2)


def flip2(v):
    return v + 2 - 4 * ((v // 2) % 2)


def flips(v):
    return (flip1(v), flip2(v), 3 - v)


def remote(src, dst, send, recv, device):
    return pltpu.make_async_remote_copy(
        src_ref=src,
        dst_ref=dst,
        send_sem=send,
        recv_sem=recv,
        device_id=device,
        device_id_type=MESH,
    )


def kernel(
    seq_hbm,
    ngain_hbm,
    bf_hbm,
    tw_hbm,
    mgain_hbm,
    gw_hbm,
    uw_hbm,
    dw_hbm,
    out_hbm,
    ngain_ref,
    mgain_ref,
    tw_ref,
    seq,
    bf,
    normed,
    zs,
    z1,
    cr,
    c1,
    ya,
    yo,
    ob,
    z2,
    wt,
    twf,
    tws,
    twr,
    twy,
    twt,
    xs,
    res,
    outb,
    seq_sem,
    bf_sem,
    small_sem,
    w_sem,
    out_sem,
    tw_send,
    tw_recv,
    ty_send,
    ty_recv,
    wz_send,
    wz_recv,
    wl_send,
    wl_recv,
    wy_send,
    wy_recv,
    wx_send,
    wx_recv,
    wc_send,
    wc_recv,
    z1_send,
    z1_recv,
    cr_send,
    cr_recv,
    ya_send,
    ya_recv,
    yo_send,
    yo_recv,
    z2_send,
    z2_recv,
):
    dp = lax.axis_index("dp")
    sq = lax.axis_index("seq")
    zl, xx = dp // XN, dp % XN
    zh, yy, cc = sq // (YN * 2), (sq // 2) % YN, sq % 2

    def place(z=None, y=None, c=None, x=None):
        z = zh if z is None else z
        y = yy if y is None else y
        c = cc if c is None else c
        x = xx if x is None else x
        return (zl * XN + x, z * (YN * 2) + y * 2 + c)

    def along(step):
        z = (zh * ZL + zl + step) % (ZH * ZL)
        return ((z % ZL) * XN + xx, (z // ZL) * (YN * 2) + sq % (YN * 2))

    piece = pl.ds(pl.multiple_of(zl * 128, 128), 128)
    zp = flips(zh)
    yp = flips(yy)
    xp = flips(xx)
    cp = 1 - cc

    barrier = pltpu.get_barrier_semaphore()
    peers = (
        [place(z=z) for z in zp]
        + [place(y=y) for y in yp]
        + [place(x=x) for x in xp]
        + [place(c=cp)]
        + [along(step) for step in (1, ZH * ZL - 1, 2, ZH * ZL - 2)]
    )
    for peer in peers:
        pl.semaphore_signal(barrier, inc=1, device_id=peer, device_id_type=MESH)

    small = []
    for i, (src, dst) in enumerate(
        ((tw_hbm, tw_ref), (ngain_hbm, ngain_ref), (mgain_hbm, mgain_ref))
    ):
        copy = pltpu.make_async_copy(src, dst, small_sem.at[i])
        copy.start()
        small.append(copy)
    seq_copies = []
    for i in range(4):
        rows = pl.ds(i * 128, 128)
        copy = pltpu.make_async_copy(seq_hbm.at[rows], seq.at[rows], seq_sem.at[i])
        copy.start()
        seq_copies.append(copy)
    bf_copy = pltpu.make_async_copy(bf_hbm.at[0], bf, bf_sem)
    bf_copy.start()
    w_copies = []
    for m, w_hbm in enumerate((gw_hbm, uw_hbm, dw_hbm)):
        copy = pltpu.make_async_copy(
            w_hbm.at[xx, :, piece],
            wt.at[xx, zh, yy, cc, pl.ds(m * 16, 16), piece],
            w_sem.at[m],
        )
        copy.start()
        w_copies.append(copy)
    for copy in small:
        copy.wait()
    for s in range(5):
        twf[pl.ds(2 * s, 2), :] = tw_ref[s].astype(F32)
    twf[pl.ds(10, 6), :] = jnp.zeros((6, ROWS), F32)
    tws[...] = twf[...].astype(BF16)
    twr[zh] = tws[:, pl.ds(pl.multiple_of(zh * 128, 128), 128)]
    for copy in w_copies:
        copy.wait()

    for i in range(4):
        seq_copies[i].wait()

        @pl.loop(0, 8, unroll=4)
        def _(j):
            rows = pl.ds(pl.multiple_of(i * 128 + j * 16, 16), 16)
            v = seq[rows, :].astype(F32)
            scale = lax.rsqrt(jnp.mean(v * v, axis=-1, keepdims=True) + 1e-6)
            normed[rows, :] = (v * scale * ngain_ref[...]).astype(BF16)

    bf_copy.wait()

    def z1_copy(c, i):
        return remote(
            zs.at[c, zp[i]], z1.at[c, zh], z1_send.at[c, i], z1_recv.at[c, i], place(z=zp[i])
        )

    def mix(c):
        lhs = jnp.concatenate(
            [bf[pl.ds(pl.multiple_of(q * 128 + c * R, R), R), :] for q in range(ZH)], axis=0
        )
        for n in range(FEAT // TILE):
            cols = pl.ds(n * TILE, TILE)
            part = jnp.dot(lhs, normed[:, cols], preferred_element_type=F32).astype(BF16)
            zs[c, :, :, cols] = part.reshape(ZH, R, TILE)
        z1[c, zh] = zs[c, zh]

    mix(0)

    pl.semaphore_wait(barrier, len(peers))

    wz, tz = [], []
    for i, z in enumerate(zp):
        own = wt.at[xx, zh, yy, cc, :, piece]
        copy = remote(own, own, wz_send.at[i], wz_recv.at[i], place(z=z))
        copy.start()
        wz.append(copy)
        copy = remote(
            tws.at[:, pl.ds(pl.multiple_of(z * 128, 128), 128)],
            twr.at[zh],
            tw_send.at[i],
            tw_recv.at[i],
            place(z=z),
        )
        copy.start()
        tz.append(copy)

    for i in range(3):
        z1_copy(0, i).start()

    @pl.loop(1, CH)
    def _(c):
        mix(c)
        for i in range(3):
            z1_copy(c, i).start()

    for copy in tz:
        copy.wait_recv()
    ty = []
    for i, y in enumerate(yp):
        copy = remote(twr, twy.at[yy], ty_send.at[i], ty_recv.at[i], place(y=y))
        copy.start()
        ty.append(copy)
    twy[yy] = twr[...]
    for copy in ty:
        copy.wait_recv()
    for h in range(2):
        twt[h] = twy[2 * h : 2 * h + 2].astype(F32).reshape(128, 128).T
    twt[2] = jnp.concatenate([twr[...].astype(F32).reshape(64, 128), jnp.zeros((64, 128), F32)], axis=0).T

    steps = (1, ZH * ZL - 1, 2)

    def z_copy(i):
        own = wt.at[xx, zh, yy, cc, :, piece]
        return remote(own, own, wz_send.at[i], wz_recv.at[i], place(z=zp[i]))

    def l_copy(i, got=False):
        cols = piece
        if got:
            cols = pl.ds(pl.multiple_of((zl + 4 * ZL - steps[i]) % ZL * 128, 128), 128)
        own = wt.at[xx, :, yy, cc, :, cols]
        return remote(own, own, wl_send.at[i], wl_recv.at[i], along(steps[i]))

    def y_copy(i):
        own = wt.at[xx, :, yy, cc]
        return remote(own, own, wy_send.at[i], wy_recv.at[i], place(y=yp[i]))

    def x_copy(i):
        own = wt.at[xx, :, :, cc]
        return remote(own, own, wx_send.at[i], wx_recv.at[i], place(x=xp[i]))

    def c_copy(c):
        return remote(z1.at[c], cr.at[c], cr_send.at[c], cr_recv.at[c], place(c=cp))

    def ya_copy(c, i):
        cols = pl.ds(pl.multiple_of(yp[i] * YC, YC), YC)
        return remote(
            c1.at[c, :, :, cols],
            ya.at[c, yy],
            ya_send.at[c, i],
            ya_recv.at[c, i],
            place(y=yp[i]),
        )

    def yo_copy(c, i):
        cols = pl.ds(pl.multiple_of(yy * YC, YC), YC)
        return remote(
            yo.at[c, yp[i]],
            ob.at[c, :, :, cols],
            yo_send.at[c, i],
            yo_recv.at[c, i],
            place(y=yp[i]),
        )

    def z2_copy(c, i):
        return remote(
            ob.at[c, zp[i]], z2.at[c, zh], z2_send.at[c, i], z2_recv.at[c, i], place(z=zp[i])
        )

    mine = pl.ds(pl.multiple_of(yy * YC, YC), YC)

    def first_section(c):
        block = twt[2, pl.ds(pl.multiple_of(c * R, R), R), :]
        for z in range(ZH):
            own, cross = block[:, 16 * z : 16 * z + 1], block[:, 16 * z + 1 : 16 * z + 2]
            for n in range(FEAT // TILE):
                cols = pl.ds(n * TILE, TILE)
                c1[c, z, :, cols] = (
                    own * z1[c, z, :, cols].astype(F32) + cross * cr[c, z, :, cols].astype(F32)
                ).astype(BF16)

    def other_sections(c):
        rows = pl.ds(pl.multiple_of(c * R, R), R)
        blocks = (twt[0, rows, :], twt[1, rows, :])

        def coefs(b, s):
            lane = (b % 8) * 16 + 2 * s
            return blocks[b // 8][:, lane : lane + 1], blocks[b // 8][:, lane + 1 : lane + 2]

        for n in range(YC // 128):
            cols = pl.ds(n * 128, 128)
            cur = [ya[c, b // ZH, b % ZH, :, cols].astype(F32) for b in range(YN * ZH)]
            for s, step in ((1, 4), (2, 8), (3, 1), (4, 2)):
                to = []
                for b in range(YN * ZH):
                    own, cross = coefs(b, s)
                    to.append((own * cur[b] + cross * cur[b ^ step]).astype(BF16))
                cur = to if s == 4 else [v.astype(F32) for v in to]
            for b in range(YN * ZH):
                yo[c, b // ZH, b % ZH, :, cols] = cur[b]

    @pl.loop(0, CH + 2)
    def _(t):
        @pl.when(t < CH)
        def _():
            for i in range(3):
                z1_copy(t, i).wait_recv()
            c_copy(t).start()

        @pl.when(t >= 2)
        def _():
            c = t - 2
            for i in range(3):
                yo_copy(c, i).wait_recv()
            for i in range(3):
                z2_copy(c, i).start()
            z2[c, zh] = ob[c, zh]

        @pl.when((t >= 1) & (t < CH + 1))
        def _():
            c = t - 1
            for i in range(3):
                ya_copy(c, i).wait_recv()
            other_sections(c)
            for i in range(3):
                yo_copy(c, i).start()
            ob[c, :, :, mine] = yo[c, yy]

        @pl.when(t < CH)
        def _():
            c_copy(t).wait_recv()
            first_section(t)
            for i in range(3):
                ya_copy(t, i).start()
            ya[t, yy] = c1[t, :, :, mine]

        @pl.when(t == 0)
        def _():
            for i in range(3):
                z_copy(i).wait_recv()
            for i in range(3):
                l_copy(i).start()

        @pl.when(t == 2)
        def _():
            for i in range(3):
                l_copy(i, True).wait_recv()
            for i in range(3):
                y_copy(i).start()

        @pl.when(t == 3)
        def _():
            for i in range(3):
                y_copy(i).wait_recv()
            for i in range(3):
                x_copy(i).start()

        @pl.when(t == 7)
        def _():
            for i in range(3):
                x_copy(i).wait_recv()
            own = wt.at[:, :, :, cc]
            remote(own, own, wc_send, wc_recv, place(c=cp)).start()

    own = wt.at[:, :, :, cc]
    w_core = remote(own, own, wc_send, wc_recv, place(c=cp))
    w_core.wait_recv()

    def weight(k, m):
        return wt[k, :, :, :, m * 16 : (m + 1) * 16, :].reshape(GRP, GRP)

    def out_copy(c, q):
        rows = pl.ds(pl.multiple_of(q * 128 + c * R, R), R)
        return pltpu.make_async_copy(outb.at[c, q], out_hbm.at[rows], out_sem.at[c, q])

    @pl.loop(0, CH)
    def _(c):
        for i in range(3):
            z2_copy(c, i).wait_recv()
        for q in range(ZH):
            rows = pl.ds(pl.multiple_of(q * 128 + c * R, R), R)
            r = (seq[rows, :].astype(F32) + z2[c, q].astype(F32)).astype(BF16)
            res[pl.ds(q * R, R), :] = r
            v = r.astype(F32)
            scale = lax.rsqrt(jnp.mean(v * v, axis=-1, keepdims=True) + 1e-6)
            xs[pl.ds(q * R, R), :] = (v * scale * mgain_ref[...]).astype(BF16)

        for k in range(FEAT // GRP):
            cols = pl.ds(k * GRP, GRP)
            x = xs[:, cols]
            gate = jnp.dot(x, weight(k, 0), preferred_element_type=F32)
            up = jnp.dot(x, weight(k, 1), preferred_element_type=F32)
            hidden = (gate / (1.0 + jnp.exp(-gate)) * up).astype(BF16)
            down = jnp.dot(hidden, weight(k, 2), preferred_element_type=F32)
            mixed = (res[:, cols].astype(F32) + down).astype(BF16)
            outb[c, :, :, cols] = mixed.reshape(ZH, R, GRP)
        for q in range(ZH):
            out_copy(c, q).start()

    for copy in wz + tz + ty:
        copy.wait_send()
    for i in range(3):
        l_copy(i).wait_send()
        y_copy(i).wait_send()
        x_copy(i).wait_send()
    w_core.wait_send()

    @pl.loop(0, CH)
    def _(c):
        for i in range(3):
            z1_copy(c, i).wait_send()
            z2_copy(c, i).wait_send()
        c_copy(c).wait_send()
        for i in range(3):
            ya_copy(c, i).wait_send()
            yo_copy(c, i).wait_send()
        for q in range(ZH):
            out_copy(c, q).wait()


def local(
    sequence, norm_gain, block_factor, twiddle, mlp_gain, gate_weight, up_weight, down_weight
):
    hbm = pl.BlockSpec(memory_space=pltpu.HBM)
    chunk = pltpu.VMEM((CH, ZH, R, FEAT), BF16)
    dma = pltpu.SemaphoreType.DMA
    return pl.pallas_call(
        kernel,
        name="monarch",
        out_shape=pltpu.VMEM((ROWS, FEAT), BF16),
        in_specs=[hbm] * 8,
        out_specs=pl.BlockSpec(memory_space=pl.ANY),
        scratch_shapes=[
            pltpu.VMEM((1, FEAT), F32),
            pltpu.VMEM((1, FEAT), F32),
            pltpu.VMEM((5, 2, ROWS), BF16),
            pltpu.VMEM((ROWS, FEAT), BF16),
            pltpu.VMEM((ROWS, ROWS), BF16),
            pltpu.VMEM((ROWS, FEAT), BF16),
            chunk,
            chunk,
            chunk,
            chunk,
            pltpu.VMEM((CH, YN, ZH, R, YC), BF16),
            pltpu.VMEM((CH, YN, ZH, R, YC), BF16),
            chunk,
            chunk,
            pltpu.VMEM((XN, ZH, YN, 2, 48, GRP), BF16),
            pltpu.VMEM((16, ROWS), F32),
            pltpu.VMEM((16, ROWS), BF16),
            pltpu.VMEM((ZH, 16, 128), BF16),
            pltpu.VMEM((YN, ZH, 16, 128), BF16),
            pltpu.VMEM((3, 128, 128), F32),
            pltpu.VMEM((ZH * R, FEAT), BF16),
            pltpu.VMEM((ZH * R, FEAT), BF16),
            chunk,
            dma((4,)),
            dma,
            dma((3,)),
            dma((3,)),
            dma((CH, ZH)),
            dma((3,)),
            dma((3,)),
            dma((3,)),
            dma((3,)),
            dma((3,)),
            dma((3,)),
            dma((3,)),
            dma((3,)),
            dma((3,)),
            dma((3,)),
            dma((3,)),
            dma((3,)),
            dma,
            dma,
            dma((CH, 3)),
            dma((CH, 3)),
            dma((CH,)),
            dma((CH,)),
            dma((CH, 3)),
            dma((CH, 3)),
            dma((CH, 3)),
            dma((CH, 3)),
            dma((CH, 3)),
            dma((CH, 3)),
        ],
        compiler_params=pltpu.CompilerParams(
            collective_id=0, has_side_effects=True, vmem_limit_bytes=56 * 1024 * 1024
        ),
        cost_estimate=pl.CostEstimate(
            flops=5 * 2**30, bytes_accessed=8 * 2**20, transcendentals=2**20
        ),
    )(
        sequence,
        norm_gain.reshape(1, FEAT),
        block_factor,
        twiddle,
        mlp_gain.reshape(1, FEAT),
        gate_weight,
        up_weight,
        down_weight,
    )


def solution(mesh):
    return jax.shard_map(
        local,
        mesh=mesh,
        in_specs=(
            P(("dp", "seq"), None),
            P(),
            P("seq", None, None),
            P(None, None, "seq"),
            P(),
            P(None, "seq", None),
            P(None, "seq", None),
            P(None, "seq", None),
        ),
        out_specs=P(("dp", "seq"), None),
        check_vma=False,
    )
```

```python
import functools

import jax
import jax.numpy as jnp
from jax import lax
from jax.experimental import pallas as pl
from jax.experimental.pallas import tpu as pltpu
from jax.sharding import PartitionSpec as P

MESH = pl.DeviceIdType.MESH
F32 = jnp.float32
BF16 = jnp.bfloat16

ZH = 4
ZL = 4
YN = 4
XN = 4
ROWS = 512
FEAT = 2048
GRP = 512
CH = 8
R = 16
TILE = 512
YC = 512


def flip1(v):
    return v + 1 - 2 * (v % 2)


def flip2(v):
    return v + 2 - 4 * ((v // 2) % 2)


def flips(v):
    return (flip1(v), flip2(v), 3 - v)


def remote(src, dst, send, recv, device):
    return pltpu.make_async_remote_copy(
        src_ref=src,
        dst_ref=dst,
        send_sem=send,
        recv_sem=recv,
        device_id=device,
        device_id_type=MESH,
    )


def kernel(
    seq_hbm,
    ngain_hbm,
    bf_hbm,
    tw_hbm,
    mgain_hbm,
    gw_hbm,
    uw_hbm,
    dw_hbm,
    out_ref,
    ngain_ref,
    mgain_ref,
    tw_ref,
    seq,
    bf,
    normed,
    zs,
    z1,
    cr,
    c1,
    ya,
    yo,
    ob,
    z2,
    wt,
    twf,
    tws,
    twr,
    twy,
    twt,
    xs,
    res,
    seq_sem,
    bf_sem,
    small_sem,
    w_sem,
    tw_send,
    tw_recv,
    ty_send,
    ty_recv,
    wz_send,
    wz_recv,
    wl_send,
    wl_recv,
    wy_send,
    wy_recv,
    wx_send,
    wx_recv,
    wc_send,
    wc_recv,
    z1_send,
    z1_recv,
    cr_send,
    cr_recv,
    ya_send,
    ya_recv,
    yo_send,
    yo_recv,
    z2_send,
    z2_recv,
):
    dp = lax.axis_index("dp")
    sq = lax.axis_index("seq")
    zl, xx = dp // XN, dp % XN
    zh, yy, cc = sq // (YN * 2), (sq // 2) % YN, sq % 2

    def place(z=None, y=None, c=None, x=None):
        z = zh if z is None else z
        y = yy if y is None else y
        c = cc if c is None else c
        x = xx if x is None else x
        return (zl * XN + x, z * (YN * 2) + y * 2 + c)

    def along(step):
        z = (zh * ZL + zl + step) % (ZH * ZL)
        return ((z % ZL) * XN + xx, (z // ZL) * (YN * 2) + sq % (YN * 2))

    piece = pl.ds(pl.multiple_of(zl * 128, 128), 128)
    zp = flips(zh)
    yp = flips(yy)
    xp = flips(xx)
    cp = 1 - cc

    barrier = pltpu.get_barrier_semaphore()
    peers = (
        [place(z=z) for z in zp]
        + [place(y=y) for y in yp]
        + [place(x=x) for x in xp]
        + [place(c=cp)]
        + [along(step) for step in (1, ZH * ZL - 1, 2, ZH * ZL - 2)]
    )
    for peer in peers:
        pl.semaphore_signal(barrier, inc=1, device_id=peer, device_id_type=MESH)

    small = []
    for i, (src, dst) in enumerate(
        ((ngain_hbm, ngain_ref), (tw_hbm, tw_ref), (mgain_hbm, mgain_ref))
    ):
        copy = pltpu.make_async_copy(src, dst, small_sem.at[i])
        copy.start()
        small.append(copy)
    seq_copies = []
    for i in range(4):
        rows = pl.ds(i * 128, 128)
        copy = pltpu.make_async_copy(seq_hbm.at[rows], seq.at[rows], seq_sem.at[i])
        copy.start()
        seq_copies.append(copy)
    bf_copy = pltpu.make_async_copy(bf_hbm.at[0], bf, bf_sem)
    bf_copy.start()
    w_copies = []
    for m, w_hbm in enumerate((gw_hbm, uw_hbm, dw_hbm)):
        copy = pltpu.make_async_copy(
            w_hbm.at[xx, :, piece],
            wt.at[xx, zh, yy, cc, pl.ds(m * 16, 16), piece],
            w_sem.at[m],
        )
        copy.start()
        w_copies.append(copy)
    small[0].wait()
    for i in range(4):
        seq_copies[i].wait()

        @pl.loop(0, 8, unroll=4)
        def _(j):
            rows = pl.ds(pl.multiple_of(i * 128 + j * 16, 16), 16)
            v = seq[rows, :].astype(F32)
            scale = lax.rsqrt(jnp.mean(v * v, axis=-1, keepdims=True) + 1e-6)
            normed[rows, :] = (v * scale * ngain_ref[...]).astype(BF16)

    bf_copy.wait()

    def z1_copy(c, i):
        return remote(
            zs.at[c, zp[i]], z1.at[c, zh], z1_send.at[c, i], z1_recv.at[c, i], place(z=zp[i])
        )

    def mix(c):
        lhs = jnp.concatenate(
            [bf[pl.ds(pl.multiple_of(q * 128 + c * R, R), R), :] for q in range(ZH)], axis=0
        )
        for n in range(FEAT // TILE):
            cols = pl.ds(n * TILE, TILE)
            part = jnp.dot(lhs, normed[:, cols], preferred_element_type=F32).astype(BF16)
            zs[c, :, :, cols] = part.reshape(ZH, R, TILE)
        z1[c, zh] = zs[c, zh]

    mix(0)
    for copy in small[1:]:
        copy.wait()
    for s in range(5):
        twf[pl.ds(2 * s, 2), :] = tw_ref[s].astype(F32)
    twf[pl.ds(10, 6), :] = jnp.zeros((6, ROWS), F32)
    tws[...] = twf[...].astype(BF16)
    twr[zh] = tws[:, pl.ds(pl.multiple_of(zh * 128, 128), 128)]
    for copy in w_copies:
        copy.wait()

    pl.semaphore_wait(barrier, len(peers))
    for i in range(3):
        z1_copy(0, i).start()

    wz, tz = [], []
    for i, z in enumerate(zp):
        own = wt.at[xx, zh, yy, cc, :, piece]
        copy = remote(own, own, wz_send.at[i], wz_recv.at[i], place(z=z))
        copy.start()
        wz.append(copy)
        copy = remote(
            tws.at[:, pl.ds(pl.multiple_of(z * 128, 128), 128)],
            twr.at[zh],
            tw_send.at[i],
            tw_recv.at[i],
            place(z=z),
        )
        copy.start()
        tz.append(copy)

    @pl.loop(1, CH)
    def _(c):
        mix(c)
        for i in range(3):
            z1_copy(c, i).start()

    for copy in tz:
        copy.wait_recv()
    ty = []
    for i, y in enumerate(yp):
        copy = remote(twr, twy.at[yy], ty_send.at[i], ty_recv.at[i], place(y=y))
        copy.start()
        ty.append(copy)
    twy[yy] = twr[...]
    for copy in ty:
        copy.wait_recv()
    for h in range(2):
        twt[h] = twy[2 * h : 2 * h + 2].astype(F32).reshape(128, 128).T
    twt[2] = jnp.concatenate([twr[...].astype(F32).reshape(64, 128), jnp.zeros((64, 128), F32)], axis=0).T

    steps = (1, ZH * ZL - 1, 2)

    def z_copy(i):
        own = wt.at[xx, zh, yy, cc, :, piece]
        return remote(own, own, wz_send.at[i], wz_recv.at[i], place(z=zp[i]))

    def l_copy(i, got=False):
        cols = piece
        if got:
            cols = pl.ds(pl.multiple_of((zl + 4 * ZL - steps[i]) % ZL * 128, 128), 128)
        own = wt.at[xx, :, yy, cc, :, cols]
        return remote(own, own, wl_send.at[i], wl_recv.at[i], along(steps[i]))

    def y_copy(i):
        own = wt.at[xx, :, yy, cc]
        return remote(own, own, wy_send.at[i], wy_recv.at[i], place(y=yp[i]))

    def x_copy(i):
        own = wt.at[xx, :, :, cc]
        return remote(own, own, wx_send.at[i], wx_recv.at[i], place(x=xp[i]))

    def c_copy(c):
        return remote(z1.at[c], cr.at[c], cr_send.at[c], cr_recv.at[c], place(c=cp))

    def ya_copy(c, i):
        cols = pl.ds(pl.multiple_of(yp[i] * YC, YC), YC)
        return remote(
            c1.at[c, :, :, cols],
            ya.at[c, yy],
            ya_send.at[c, i],
            ya_recv.at[c, i],
            place(y=yp[i]),
        )

    def yo_copy(c, i):
        cols = pl.ds(pl.multiple_of(yy * YC, YC), YC)
        return remote(
            yo.at[c, yp[i]],
            ob.at[c, :, :, cols],
            yo_send.at[c, i],
            yo_recv.at[c, i],
            place(y=yp[i]),
        )

    def z2_copy(c, i):
        return remote(
            ob.at[c, zp[i]], z2.at[c, zh], z2_send.at[c, i], z2_recv.at[c, i], place(z=zp[i])
        )

    mine = pl.ds(pl.multiple_of(yy * YC, YC), YC)

    def first_section(c):
        block = twt[2, pl.ds(pl.multiple_of(c * R, R), R), :]
        for z in range(ZH):
            own, cross = block[:, 16 * z : 16 * z + 1], block[:, 16 * z + 1 : 16 * z + 2]
            for n in range(FEAT // TILE):
                cols = pl.ds(n * TILE, TILE)
                c1[c, z, :, cols] = (
                    own * z1[c, z, :, cols].astype(F32) + cross * cr[c, z, :, cols].astype(F32)
                ).astype(BF16)

    def other_sections(c):
        rows = pl.ds(pl.multiple_of(c * R, R), R)
        blocks = (twt[0, rows, :], twt[1, rows, :])

        def coefs(b, s):
            lane = (b % 8) * 16 + 2 * s
            return blocks[b // 8][:, lane : lane + 1], blocks[b // 8][:, lane + 1 : lane + 2]

        for n in range(YC // 128):
            cols = pl.ds(n * 128, 128)
            cur = [ya[c, b // ZH, b % ZH, :, cols].astype(F32) for b in range(YN * ZH)]
            for s, step in ((1, 4), (2, 8), (3, 1), (4, 2)):
                to = []
                for b in range(YN * ZH):
                    own, cross = coefs(b, s)
                    to.append((own * cur[b] + cross * cur[b ^ step]).astype(BF16))
                cur = to if s == 4 else [v.astype(F32) for v in to]
            for b in range(YN * ZH):
                yo[c, b // ZH, b % ZH, :, cols] = cur[b]

    @pl.loop(0, CH + 1)
    def _(t):
        @pl.when(t < CH)
        def _():
            for i in range(3):
                z1_copy(t, i).wait_recv()
            c_copy(t).start()
            c_copy(t).wait_recv()
            first_section(t)
            for i in range(3):
                ya_copy(t, i).start()
            ya[t, yy] = c1[t, :, :, mine]

        @pl.when(t >= 1)
        def _():
            c = t - 1
            for i in range(3):
                yo_copy(c, i).wait_recv()
            for i in range(3):
                z2_copy(c, i).start()
            z2[c, zh] = ob[c, zh]

        @pl.when(t < CH)
        def _():
            for i in range(3):
                ya_copy(t, i).wait_recv()
            other_sections(t)
            for i in range(3):
                yo_copy(t, i).start()
            ob[t, :, :, mine] = yo[t, yy]

        @pl.when(t == 0)
        def _():
            for i in range(3):
                z_copy(i).wait_recv()
            for i in range(3):
                l_copy(i).start()

        @pl.when(t == 2)
        def _():
            for i in range(3):
                l_copy(i, True).wait_recv()
            for i in range(3):
                y_copy(i).start()

        @pl.when(t == 3)
        def _():
            for i in range(3):
                y_copy(i).wait_recv()
            for i in range(3):
                x_copy(i).start()

        @pl.when(t == CH)
        def _():
            for i in range(3):
                x_copy(i).wait_recv()
            own = wt.at[:, :, :, cc]
            remote(own, own, wc_send, wc_recv, place(c=cp)).start()

    own = wt.at[:, :, :, cc]
    w_core = remote(own, own, wc_send, wc_recv, place(c=cp))
    w_core.wait_recv()

    def weight(k, m):
        return wt[k, :, :, :, m * 16 : (m + 1) * 16, :].reshape(GRP, GRP)

    @pl.loop(0, CH)
    def _(c):
        for i in range(3):
            z2_copy(c, i).wait_recv()
        for q in range(ZH):
            rows = pl.ds(pl.multiple_of(q * 128 + c * R, R), R)
            r = (seq[rows, :].astype(F32) + z2[c, q].astype(F32)).astype(BF16)
            res[pl.ds(q * R, R), :] = r
            v = r.astype(F32)
            scale = lax.rsqrt(jnp.mean(v * v, axis=-1, keepdims=True) + 1e-6)
            xs[pl.ds(q * R, R), :] = (v * scale * mgain_ref[...]).astype(BF16)

        for k in range(FEAT // GRP):
            cols = pl.ds(k * GRP, GRP)
            x = xs[:, cols]
            gate = jnp.dot(x, weight(k, 0), preferred_element_type=F32)
            up = jnp.dot(x, weight(k, 1), preferred_element_type=F32)
            hidden = (gate / (1.0 + jnp.exp(-gate)) * up).astype(BF16)
            down = jnp.dot(hidden, weight(k, 2), preferred_element_type=F32)
            mixed = (res[:, cols].astype(F32) + down).astype(BF16)
            for q in range(ZH):
                rows = pl.ds(pl.multiple_of(q * 128 + c * R, R), R)
                out_ref[rows, cols] = mixed[q * R : (q + 1) * R]

    for copy in wz + tz + ty:
        copy.wait_send()
    for i in range(3):
        l_copy(i).wait_send()
        y_copy(i).wait_send()
        x_copy(i).wait_send()
    w_core.wait_send()

    @pl.loop(0, CH)
    def _(c):
        for i in range(3):
            z1_copy(c, i).wait_send()
            z2_copy(c, i).wait_send()
        c_copy(c).wait_send()
        for i in range(3):
            ya_copy(c, i).wait_send()
            yo_copy(c, i).wait_send()


def local(
    sequence, norm_gain, block_factor, twiddle, mlp_gain, gate_weight, up_weight, down_weight
):
    hbm = pl.BlockSpec(memory_space=pltpu.HBM)
    chunk = pltpu.VMEM((CH, ZH, R, FEAT), BF16)
    dma = pltpu.SemaphoreType.DMA
    return pl.pallas_call(
        kernel,
        name="monarch",
        out_shape=pltpu.VMEM((ROWS, FEAT), BF16),
        in_specs=[hbm] * 8,
        out_specs=pl.BlockSpec(memory_space=pltpu.VMEM),
        scratch_shapes=[
            pltpu.VMEM((1, FEAT), F32),
            pltpu.VMEM((1, FEAT), F32),
            pltpu.VMEM((5, 2, ROWS), BF16),
            pltpu.VMEM((ROWS, FEAT), BF16),
            pltpu.VMEM((ROWS, ROWS), BF16),
            pltpu.VMEM((ROWS, FEAT), BF16),
            chunk,
            chunk,
            chunk,
            chunk,
            pltpu.VMEM((CH, YN, ZH, R, YC), BF16),
            pltpu.VMEM((CH, YN, ZH, R, YC), BF16),
            chunk,
            chunk,
            pltpu.VMEM((XN, ZH, YN, 2, 48, GRP), BF16),
            pltpu.VMEM((16, ROWS), F32),
            pltpu.VMEM((16, ROWS), BF16),
            pltpu.VMEM((ZH, 16, 128), BF16),
            pltpu.VMEM((YN, ZH, 16, 128), BF16),
            pltpu.VMEM((3, 128, 128), F32),
            pltpu.VMEM((ZH * R, FEAT), BF16),
            pltpu.VMEM((ZH * R, FEAT), BF16),
            dma((4,)),
            dma,
            dma((3,)),
            dma((3,)),
            dma((3,)),
            dma((3,)),
            dma((3,)),
            dma((3,)),
            dma((3,)),
            dma((3,)),
            dma((3,)),
            dma((3,)),
            dma((3,)),
            dma((3,)),
            dma((3,)),
            dma((3,)),
            dma,
            dma,
            dma((CH, 3)),
            dma((CH, 3)),
            dma((CH,)),
            dma((CH,)),
            dma((CH, 3)),
            dma((CH, 3)),
            dma((CH, 3)),
            dma((CH, 3)),
            dma((CH, 3)),
            dma((CH, 3)),
        ],
        compiler_params=pltpu.CompilerParams(
            collective_id=0, has_side_effects=True, vmem_limit_bytes=56 * 1024 * 1024
        ),
        cost_estimate=pl.CostEstimate(
            flops=5 * 2**30, bytes_accessed=8 * 2**20, transcendentals=2**20
        ),
    )(
        sequence,
        norm_gain.reshape(1, FEAT),
        block_factor,
        twiddle,
        mlp_gain.reshape(1, FEAT),
        gate_weight,
        up_weight,
        down_weight,
    )


def solution(mesh):
    return jax.shard_map(
        local,
        mesh=mesh,
        in_specs=(
            P(("dp", "seq"), None),
            P(),
            P("seq", None, None),
            P(None, None, "seq"),
            P(),
            P(None, "seq", None),
            P(None, "seq", None),
            P(None, "seq", None),
        ),
        out_specs=P(("dp", "seq"), None),
        check_vma=False,
    )
```

```python
import functools

import jax
import jax.numpy as jnp
from jax import lax
from jax.experimental import pallas as pl
from jax.experimental.pallas import tpu as pltpu
from jax.sharding import PartitionSpec as P

MESH = pl.DeviceIdType.MESH
F32 = jnp.float32
BF16 = jnp.bfloat16

ZH = 4
ZL = 4
YN = 4
XN = 4
ROWS = 512
FEAT = 2048
GRP = 512
CH = 8
R = 16
TILE = 512
YC = 512


def flip1(v):
    return v + 1 - 2 * (v % 2)


def flip2(v):
    return v + 2 - 4 * ((v // 2) % 2)


def flips(v):
    return (flip1(v), flip2(v), 3 - v)


def remote(src, dst, send, recv, device):
    return pltpu.make_async_remote_copy(
        src_ref=src,
        dst_ref=dst,
        send_sem=send,
        recv_sem=recv,
        device_id=device,
        device_id_type=MESH,
    )


def kernel(
    seq_hbm,
    ngain_hbm,
    bf_hbm,
    tw_hbm,
    mgain_hbm,
    gw_hbm,
    uw_hbm,
    dw_hbm,
    out_ref,
    ngain_ref,
    mgain_ref,
    tw_ref,
    seq,
    bf,
    normed,
    zs,
    z1,
    cr,
    c1,
    ya,
    yo,
    ob,
    z2,
    wt,
    twf,
    tws,
    twr,
    twy,
    twt,
    xs,
    res,
    seq_sem,
    bf_sem,
    small_sem,
    w_sem,
    tw_send,
    tw_recv,
    ty_send,
    ty_recv,
    wz_send,
    wz_recv,
    wl_send,
    wl_recv,
    wy_send,
    wy_recv,
    wx_send,
    wx_recv,
    wc_send,
    wc_recv,
    z1_send,
    z1_recv,
    cr_send,
    cr_recv,
    ya_send,
    ya_recv,
    yo_send,
    yo_recv,
    z2_send,
    z2_recv,
):
    dp = lax.axis_index("dp")
    sq = lax.axis_index("seq")
    zl, xx = dp // XN, dp % XN
    zh, yy, cc = sq // (YN * 2), (sq // 2) % YN, sq % 2

    def place(z=None, y=None, c=None, x=None):
        z = zh if z is None else z
        y = yy if y is None else y
        c = cc if c is None else c
        x = xx if x is None else x
        return (zl * XN + x, z * (YN * 2) + y * 2 + c)

    def along(step):
        z = (zh * ZL + zl + step) % (ZH * ZL)
        return ((z % ZL) * XN + xx, (z // ZL) * (YN * 2) + sq % (YN * 2))

    piece = pl.ds(pl.multiple_of(zl * 128, 128), 128)
    zp = (flip2(zh), flip1(zh), 3 - zh)
    yp = flips(yy)
    xp = flips(xx)
    cp = 1 - cc

    barrier = pltpu.get_barrier_semaphore()
    peers = (
        [place(z=z) for z in zp]
        + [place(y=y) for y in yp]
        + [place(x=x) for x in xp]
        + [place(c=cp)]
        + [along(step) for step in (1, ZH * ZL - 1, 2, ZH * ZL - 2)]
    )
    for peer in peers:
        pl.semaphore_signal(barrier, inc=1, device_id=peer, device_id_type=MESH)

    small = []
    for i, (src, dst) in enumerate(
        ((ngain_hbm, ngain_ref), (tw_hbm, tw_ref), (mgain_hbm, mgain_ref))
    ):
        copy = pltpu.make_async_copy(src, dst, small_sem.at[i])
        copy.start()
        small.append(copy)
    seq_copies = []
    for i in range(4):
        rows = pl.ds(i * 128, 128)
        copy = pltpu.make_async_copy(seq_hbm.at[rows], seq.at[rows], seq_sem.at[i])
        copy.start()
        seq_copies.append(copy)
    bf_copy = pltpu.make_async_copy(bf_hbm.at[0], bf, bf_sem)
    bf_copy.start()
    w_copies = []
    for m, w_hbm in enumerate((gw_hbm, uw_hbm, dw_hbm)):
        copy = pltpu.make_async_copy(
            w_hbm.at[xx, :, piece],
            wt.at[xx, zh, yy, cc, pl.ds(m * 16, 16), piece],
            w_sem.at[m],
        )
        copy.start()
        w_copies.append(copy)
    small[0].wait()
    for i in range(4):
        seq_copies[i].wait()

        @pl.loop(0, 8, unroll=4)
        def _(j):
            rows = pl.ds(pl.multiple_of(i * 128 + j * 16, 16), 16)
            v = seq[rows, :].astype(F32)
            scale = lax.rsqrt(jnp.mean(v * v, axis=-1, keepdims=True) + 1e-6)
            normed[rows, :] = (v * scale * ngain_ref[...]).astype(BF16)

    bf_copy.wait()

    def z1_copy(c, i):
        return remote(
            zs.at[c, zp[i]], z1.at[c, zh], z1_send.at[c, i], z1_recv.at[c, i], place(z=zp[i])
        )

    def mix(c):
        lhs = jnp.concatenate(
            [bf[pl.ds(pl.multiple_of(q * 128 + c * R, R), R), :] for q in range(ZH)], axis=0
        )
        for n in range(FEAT // TILE):
            cols = pl.ds(n * TILE, TILE)
            part = jnp.dot(lhs, normed[:, cols], preferred_element_type=F32).astype(BF16)
            zs[c, :, :, cols] = part.reshape(ZH, R, TILE)
        z1[c, zh] = zs[c, zh]

    mix(0)
    for copy in small[1:]:
        copy.wait()
    for s in range(5):
        twf[pl.ds(2 * s, 2), :] = tw_ref[s].astype(F32)
    twf[pl.ds(10, 6), :] = jnp.zeros((6, ROWS), F32)
    tws[...] = twf[...].astype(BF16)
    twr[zh] = tws[:, pl.ds(pl.multiple_of(zh * 128, 128), 128)]
    for copy in w_copies:
        copy.wait()

    pl.semaphore_wait(barrier, len(peers))
    for i in range(3):
        z1_copy(0, i).start()

    wz, tz = [], []
    for i, z in enumerate(zp):
        own = wt.at[xx, zh, yy, cc, :, piece]
        copy = remote(own, own, wz_send.at[i], wz_recv.at[i], place(z=z))
        copy.start()
        wz.append(copy)
        copy = remote(
            tws.at[:, pl.ds(pl.multiple_of(z * 128, 128), 128)],
            twr.at[zh],
            tw_send.at[i],
            tw_recv.at[i],
            place(z=z),
        )
        copy.start()
        tz.append(copy)

    @pl.loop(1, CH)
    def _(c):
        mix(c)
        for i in range(3):
            z1_copy(c, i).start()

    for copy in tz:
        copy.wait_recv()
    ty = []
    for i, y in enumerate(yp):
        copy = remote(twr, twy.at[yy], ty_send.at[i], ty_recv.at[i], place(y=y))
        copy.start()
        ty.append(copy)
    twy[yy] = twr[...]
    for copy in ty:
        copy.wait_recv()
    for h in range(2):
        twt[h] = twy[2 * h : 2 * h + 2].astype(F32).reshape(128, 128).T
    twt[2] = jnp.concatenate([twr[...].astype(F32).reshape(64, 128), jnp.zeros((64, 128), F32)], axis=0).T

    steps = (1, ZH * ZL - 1, 2)

    def z_copy(i):
        own = wt.at[xx, zh, yy, cc, :, piece]
        return remote(own, own, wz_send.at[i], wz_recv.at[i], place(z=zp[i]))

    def l_copy(i, got=False):
        cols = piece
        if got:
            cols = pl.ds(pl.multiple_of((zl + 4 * ZL - steps[i]) % ZL * 128, 128), 128)
        own = wt.at[xx, :, yy, cc, :, cols]
        return remote(own, own, wl_send.at[i], wl_recv.at[i], along(steps[i]))

    def y_copy(i):
        own = wt.at[xx, :, yy, cc]
        return remote(own, own, wy_send.at[i], wy_recv.at[i], place(y=yp[i]))

    def x_copy(i):
        own = wt.at[xx, :, :, cc]
        return remote(own, own, wx_send.at[i], wx_recv.at[i], place(x=xp[i]))

    def c_copy(c):
        return remote(z1.at[c], cr.at[c], cr_send.at[c], cr_recv.at[c], place(c=cp))

    def ya_copy(c, i):
        cols = pl.ds(pl.multiple_of(yp[i] * YC, YC), YC)
        return remote(
            c1.at[c, :, :, cols],
            ya.at[c, yy],
            ya_send.at[c, i],
            ya_recv.at[c, i],
            place(y=yp[i]),
        )

    def yo_copy(c, i):
        cols = pl.ds(pl.multiple_of(yy * YC, YC), YC)
        return remote(
            yo.at[c, yp[i]],
            ob.at[c, :, :, cols],
            yo_send.at[c, i],
            yo_recv.at[c, i],
            place(y=yp[i]),
        )

    def z2_copy(c, i):
        return remote(
            ob.at[c, zp[i]], z2.at[c, zh], z2_send.at[c, i], z2_recv.at[c, i], place(z=zp[i])
        )

    mine = pl.ds(pl.multiple_of(yy * YC, YC), YC)

    def first_section(c):
        block = twt[2, pl.ds(pl.multiple_of(c * R, R), R), :]
        for z in range(ZH):
            own, cross = block[:, 16 * z : 16 * z + 1], block[:, 16 * z + 1 : 16 * z + 2]
            for n in range(FEAT // TILE):
                cols = pl.ds(n * TILE, TILE)
                c1[c, z, :, cols] = (
                    own * z1[c, z, :, cols].astype(F32) + cross * cr[c, z, :, cols].astype(F32)
                ).astype(BF16)

    def other_sections(c):
        rows = pl.ds(pl.multiple_of(c * R, R), R)
        blocks = (twt[0, rows, :], twt[1, rows, :])

        def coefs(b, s):
            lane = (b % 8) * 16 + 2 * s
            return blocks[b // 8][:, lane : lane + 1], blocks[b // 8][:, lane + 1 : lane + 2]

        for n in range(YC // 128):
            cols = pl.ds(n * 128, 128)
            cur = [ya[c, b // ZH, b % ZH, :, cols].astype(F32) for b in range(YN * ZH)]
            for s, step in ((1, 4), (2, 8), (3, 1), (4, 2)):
                to = []
                for b in range(YN * ZH):
                    own, cross = coefs(b, s)
                    to.append((own * cur[b] + cross * cur[b ^ step]).astype(BF16))
                cur = to if s == 4 else [v.astype(F32) for v in to]
            for b in range(YN * ZH):
                yo[c, b // ZH, b % ZH, :, cols] = cur[b]

    @pl.loop(0, CH + 1)
    def _(t):
        @pl.when(t < CH)
        def _():
            for i in range(3):
                z1_copy(t, i).wait_recv()
            c_copy(t).start()
            c_copy(t).wait_recv()
            first_section(t)
            for i in range(3):
                ya_copy(t, i).start()
            ya[t, yy] = c1[t, :, :, mine]

        @pl.when(t >= 1)
        def _():
            c = t - 1
            for i in range(3):
                yo_copy(c, i).wait_recv()
            for i in range(3):
                z2_copy(c, i).start()
            z2[c, zh] = ob[c, zh]

        @pl.when(t < CH)
        def _():
            for i in range(3):
                ya_copy(t, i).wait_recv()
            other_sections(t)
            for i in range(3):
                yo_copy(t, i).start()
            ob[t, :, :, mine] = yo[t, yy]

        @pl.when(t == 0)
        def _():
            for i in range(3):
                z_copy(i).wait_recv()
            for i in range(3):
                l_copy(i).start()

        @pl.when(t == 3)
        def _():
            for i in range(3):
                l_copy(i, True).wait_recv()
            for i in range(3):
                y_copy(i).start()

        @pl.when(t == 4)
        def _():
            for i in range(3):
                y_copy(i).wait_recv()
            for i in range(3):
                x_copy(i).start()

        @pl.when(t == CH)
        def _():
            for i in range(3):
                x_copy(i).wait_recv()
            own = wt.at[:, :, :, cc]
            remote(own, own, wc_send, wc_recv, place(c=cp)).start()

    own = wt.at[:, :, :, cc]
    w_core = remote(own, own, wc_send, wc_recv, place(c=cp))
    w_core.wait_recv()

    def weight(k, m):
        return wt[k, :, :, :, m * 16 : (m + 1) * 16, :].reshape(GRP, GRP)

    @pl.loop(0, CH)
    def _(c):
        for i in range(3):
            z2_copy(c, i).wait_recv()
        for q in range(ZH):
            rows = pl.ds(pl.multiple_of(q * 128 + c * R, R), R)
            r = (seq[rows, :].astype(F32) + z2[c, q].astype(F32)).astype(BF16)
            res[pl.ds(q * R, R), :] = r
            v = r.astype(F32)
            scale = lax.rsqrt(jnp.mean(v * v, axis=-1, keepdims=True) + 1e-6)
            xs[pl.ds(q * R, R), :] = (v * scale * mgain_ref[...]).astype(BF16)

        for k in range(FEAT // GRP):
            cols = pl.ds(k * GRP, GRP)
            x = xs[:, cols]
            gate = jnp.dot(x, weight(k, 0), preferred_element_type=F32)
            up = jnp.dot(x, weight(k, 1), preferred_element_type=F32)
            hidden = (gate / (1.0 + jnp.exp(-gate)) * up).astype(BF16)
            down = jnp.dot(hidden, weight(k, 2), preferred_element_type=F32)
            mixed = (res[:, cols].astype(F32) + down).astype(BF16)
            for q in range(ZH):
                rows = pl.ds(pl.multiple_of(q * 128 + c * R, R), R)
                out_ref[rows, cols] = mixed[q * R : (q + 1) * R]

    for copy in wz + tz + ty:
        copy.wait_send()
    for i in range(3):
        l_copy(i).wait_send()
        y_copy(i).wait_send()
        x_copy(i).wait_send()
    w_core.wait_send()

    @pl.loop(0, CH)
    def _(c):
        for i in range(3):
            z1_copy(c, i).wait_send()
            z2_copy(c, i).wait_send()
        c_copy(c).wait_send()
        for i in range(3):
            ya_copy(c, i).wait_send()
            yo_copy(c, i).wait_send()


def local(
    sequence, norm_gain, block_factor, twiddle, mlp_gain, gate_weight, up_weight, down_weight
):
    hbm = pl.BlockSpec(memory_space=pltpu.HBM)
    chunk = pltpu.VMEM((CH, ZH, R, FEAT), BF16)
    dma = pltpu.SemaphoreType.DMA
    return pl.pallas_call(
        kernel,
        name="monarch",
        out_shape=pltpu.VMEM((ROWS, FEAT), BF16),
        in_specs=[hbm] * 8,
        out_specs=pl.BlockSpec(memory_space=pltpu.VMEM),
        scratch_shapes=[
            pltpu.VMEM((1, FEAT), F32),
            pltpu.VMEM((1, FEAT), F32),
            pltpu.VMEM((5, 2, ROWS), BF16),
            pltpu.VMEM((ROWS, FEAT), BF16),
            pltpu.VMEM((ROWS, ROWS), BF16),
            pltpu.VMEM((ROWS, FEAT), BF16),
            chunk,
            chunk,
            chunk,
            chunk,
            pltpu.VMEM((CH, YN, ZH, R, YC), BF16),
            pltpu.VMEM((CH, YN, ZH, R, YC), BF16),
            chunk,
            chunk,
            pltpu.VMEM((XN, ZH, YN, 2, 48, GRP), BF16),
            pltpu.VMEM((16, ROWS), F32),
            pltpu.VMEM((16, ROWS), BF16),
            pltpu.VMEM((ZH, 16, 128), BF16),
            pltpu.VMEM((YN, ZH, 16, 128), BF16),
            pltpu.VMEM((3, 128, 128), F32),
            pltpu.VMEM((ZH * R, FEAT), BF16),
            pltpu.VMEM((ZH * R, FEAT), BF16),
            dma((4,)),
            dma,
            dma((3,)),
            dma((3,)),
            dma((3,)),
            dma((3,)),
            dma((3,)),
            dma((3,)),
            dma((3,)),
            dma((3,)),
            dma((3,)),
            dma((3,)),
            dma((3,)),
            dma((3,)),
            dma((3,)),
            dma((3,)),
            dma,
            dma,
            dma((CH, 3)),
            dma((CH, 3)),
            dma((CH,)),
            dma((CH,)),
            dma((CH, 3)),
            dma((CH, 3)),
            dma((CH, 3)),
            dma((CH, 3)),
            dma((CH, 3)),
            dma((CH, 3)),
        ],
        compiler_params=pltpu.CompilerParams(
            collective_id=0, has_side_effects=True, vmem_limit_bytes=56 * 1024 * 1024
        ),
        cost_estimate=pl.CostEstimate(
            flops=5 * 2**30, bytes_accessed=8 * 2**20, transcendentals=2**20
        ),
    )(
        sequence,
        norm_gain.reshape(1, FEAT),
        block_factor,
        twiddle,
        mlp_gain.reshape(1, FEAT),
        gate_weight,
        up_weight,
        down_weight,
    )


def solution(mesh):
    return jax.shard_map(
        local,
        mesh=mesh,
        in_specs=(
            P(("dp", "seq"), None),
            P(),
            P("seq", None, None),
            P(None, None, "seq"),
            P(),
            P(None, "seq", None),
            P(None, "seq", None),
            P(None, "seq", None),
        ),
        out_specs=P(("dp", "seq"), None),
        check_vma=False,
    )
```
